32 devices in a mesh: dp: 4 (over x, core), point: 8 (over z, y).
Axes of the slice: x: 2, y: 2, z: 4, core: 2. Of those that a mesh axis runs over, the one named last changes fastest.
Arguments:
- points: bfloat16 [262144, 256], P(('dp', 'point')), parts along dimension 0, may hold values from -6 to 6
- tree_order: int32 [262144], P(('dp', 'point')), parts along dimension 0, may hold values from 0 to 65535, as said below
- ball_counts: int32 [1024], P(('dp', 'point')), parts along dimension 0, may hold values from 64 to 256, as said below
- ball_proj: bfloat16 [3, 256, 256], replicated
- ball_out: bfloat16 [256, 256], replicated, may hold values from -0.375 to 0.375
- pool_weight: bfloat16 [16384, 256], replicated, may hold values from -0.046875 to 0.046875
- coarse_proj: bfloat16 [3, 256, 256], replicated
- coarse_out: bfloat16 [256, 256], replicated, may hold values from -6 to 6
- global_proj: bfloat16 [3, 256, 256], replicated
- global_out: bfloat16 [256, 256], replicated, may hold values from -6 to 6
- unpool_weight: bfloat16 [256, 16384], replicated, may hold values from -0.125 to 0.125
- mlp_in: bfloat16 [256, 1024], replicated, may hold values from -0.375 to 0.375
- mlp_out: bfloat16 [1024, 256], replicated, may hold values from -0.1875 to 0.1875
Outputs:
- result: bfloat16 [262144, 256], P(('dp', 'point')), parts along dimension 0
The draws below stay inside these ranges and needn't reach their ends.
There are 4 independent parts, one for each index of `dp`. The reference program is written for one: setup_inputs(seed, part) draws one part's arguments, and reference() takes and returns one part's arrays. A program takes and returns all parts, laid end to end along the dimension named above; an argument that names none is the same for every part. Nothing has to cross between parts.
Inputs may be any that keep to these rules, and one draw needn't show every extreme that they name: `tree_order`: each block of 8192 slots takes a permutation of the same block of rows. `ball_counts`: live points come first in each ball; every block of 8192 slots holds a full ball.
All inputs are finite; a program needn't handle non-finite values.
Results may differ from the reference program's by a relative error of at most 0.03.
Values may be sent and summed in bfloat16 or wider, within the bound.
A program may use at most 256 MiB of HBM per device.

```python
import math
import jax
import jax.numpy as jnp
import numpy as np
from jax import lax

D = 256
HEADS = 8
FF = 1024
BALL = 256
POOL = 64
TOK_DEV = 8192
TOKENS = 65536
COARSE_DEV = 128
COARSE = 1024
LEVELS = 3
N_POINT = 8


def draw_tree_order(key, part):
    blocks = TOKENS // TOK_DEV
    key_list = jax.random.split(jax.random.fold_in(key, 11), blocks)
    local_order = jax.vmap(lambda subkey: jax.random.permutation(subkey, TOK_DEV))(key_list)
    offsets = (jnp.arange(blocks) * TOK_DEV)[:, None]
    return (local_order + offsets).reshape(-1).astype(jnp.int32)


def draw_ball_counts(key, part):
    blocks = TOKENS // TOK_DEV
    per_block = TOK_DEV // BALL
    first, second = jax.random.split(jax.random.fold_in(key, 12))
    drawn = jax.random.randint(first, (blocks, per_block), BALL // 4, BALL + 1)
    chosen = jax.random.randint(second, (blocks, 1), 0, per_block)
    full_ball = jnp.arange(per_block)[None, :] == chosen
    return jnp.where(full_ball, BALL, drawn).reshape(-1).astype(jnp.int32)


def projection_draw(key, salt):
    first, second, third = jax.random.split(jax.random.fold_in(key, salt), 3)
    factor = 1.0 / math.sqrt(D)
    shared = jax.random.normal(first, (D, D), jnp.float32) * factor
    other = jax.random.normal(second, (D, D), jnp.float32) * factor
    values = jax.random.normal(third, (D, D), jnp.float32) * factor
    q_part = shared
    k_part = other
    return jnp.stack([q_part, k_part, values]).astype(jnp.bfloat16)


def draw_ball_proj(key, part):
    return projection_draw(key, 21)


def draw_coarse_proj(key, part):
    return projection_draw(key, 22)


def draw_global_proj(key, part):
    return projection_draw(key, 23)


def shard_levels(rng, shape, cuts, low, largest):
    gain, own = 1.0, jax.random.fold_in(rng, 6)
    for axis_at, parts in cuts:
        draws = jnp.exp(jax.random.uniform(jax.random.fold_in(own, axis_at), (parts,), jnp.float32, low / len(cuts), largest / len(cuts)))
        gain = gain * jnp.repeat(draws, shape[axis_at] // parts).reshape([-1 if axis == axis_at else 1 for axis in range(len(shape))])
    return gain


def scatter_about(stream_key, extent, deviation, bound, cuts=(), kind=jnp.bfloat16):
    gain = shard_levels(stream_key, extent, cuts, -0.22, 0.18) if cuts else 1.0
    result = jax.random.normal(stream_key, extent, jnp.float32) * deviation * gain
    return jnp.minimum(jnp.maximum(result, -bound), bound).astype(kind)


def setup_inputs(seed: int = 0, part: int = 0) -> dict:
    keys = jax.random.split(jax.random.key(seed), 14)
    part_keys = jax.random.split(jax.random.fold_in(keys[13], part), 14)
    points = scatter_about(part_keys[0], (TOKENS, D), 1.0, 6.0, ((0, 8),))
    tree_order = draw_tree_order(jax.random.fold_in(jax.random.fold_in(keys[13], part), 71), part)
    ball_counts = draw_ball_counts(jax.random.fold_in(jax.random.fold_in(keys[13], part), 71), part)
    ball_proj = draw_ball_proj(jax.random.fold_in(keys[13], 71), part)
    ball_out = scatter_about(keys[4], (D, D), D ** -0.5, 0.375)
    pool_weight = scatter_about(keys[5], (POOL * D, D), (POOL * D) ** -0.5, 0.046875)
    coarse_proj = draw_coarse_proj(jax.random.fold_in(keys[13], 71), part)
    coarse_out = scatter_about(keys[7], (D, D), ((2 * COARSE_DEV / D) ** 0.5), 6.0)
    global_proj = draw_global_proj(jax.random.fold_in(keys[13], 71), part)
    global_out = scatter_about(keys[9], (D, D), (0.5 * (COARSE / D) ** 0.5), 6.0)
    unpool_weight = scatter_about(keys[10], (D, POOL * D), ((8 / COARSE_DEV) ** 0.75 / D ** 0.5), 0.125)
    mlp_in = scatter_about(keys[11], (D, FF), D ** -0.5, 0.375)
    mlp_out = scatter_about(keys[12], (FF, D), FF ** -0.5, 0.1875)
    return dict(points=points, tree_order=tree_order, ball_counts=ball_counts, ball_proj=ball_proj, ball_out=ball_out, pool_weight=pool_weight, coarse_proj=coarse_proj, coarse_out=coarse_out, global_proj=global_proj, global_out=global_out, unpool_weight=unpool_weight, mlp_in=mlp_in, mlp_out=mlp_out)


EPSILON = 1e-05

def normalize(inputs):
    inputs = inputs.astype(jnp.float32)
    center = inputs - lax.optimization_barrier(jnp.mean(inputs, axis=-1, keepdims=True))
    spread = lax.optimization_barrier(jnp.mean(center * center, axis=-1, keepdims=True))
    return (center * lax.rsqrt(spread + EPSILON)).astype(jnp.bfloat16)

def project(inputs, weight):
    return jnp.dot(inputs, weight, preferred_element_type=jnp.float32).astype(jnp.bfloat16)

def attend(queries, key_rows, value_rows, valid, head_count):
    groups, q_rows, feature = queries.shape
    k_rows = key_rows.shape[1]
    head_size = feature // head_count
    q_heads = queries.astype(jnp.float32).reshape(groups, q_rows, head_count, head_size)
    k_heads = key_rows.astype(jnp.float32).reshape(groups, k_rows, head_count, head_size)
    v_heads = value_rows.astype(jnp.float32).reshape(groups, k_rows, head_count, head_size)
    scores = jnp.einsum('bqhd,bkhd->bhqk', q_heads, k_heads) / math.sqrt(head_size)
    if valid is not None:
        scores = jnp.where(valid[:, None, None, :], scores, -1e+30)
    row_max = lax.optimization_barrier(jnp.max(scores, axis=-1, keepdims=True))
    expo = jnp.exp(scores - row_max)
    attn_probs = (expo / lax.optimization_barrier(jnp.sum(expo, axis=-1, keepdims=True))).astype(jnp.bfloat16)
    mixed = jnp.einsum('bhqk,bkhd->bqhd', attn_probs.astype(jnp.float32), v_heads)
    return mixed.reshape(groups, q_rows, feature).astype(jnp.bfloat16)

def ball_section(tree_rows, live_mask, ball_proj, ball_out):
    row_count, feature = tree_rows.shape
    normed = normalize(tree_rows)
    queries = project(normed, ball_proj[0])
    key_rows = project(normed, ball_proj[1])
    value_rows = project(normed, ball_proj[2])
    groups = row_count // BALL
    mixed = attend(queries.reshape(groups, BALL, feature), key_rows.reshape(groups, BALL, feature), value_rows.reshape(groups, BALL, feature), live_mask.reshape(groups, BALL), HEADS)
    fine = tree_rows.astype(jnp.float32) + jnp.dot(mixed.reshape(row_count, feature), ball_out, preferred_element_type=jnp.float32)
    return fine.astype(jnp.bfloat16)

def fine_section(tree_rows, live_mask, ball_proj, ball_out, pool_weight, mlp_in, mlp_out):
    row_count, feature = tree_rows.shape
    fine = ball_section(tree_rows, live_mask, ball_proj, ball_out)
    masked = jnp.where(live_mask[:, None], fine, jnp.zeros((), jnp.bfloat16))
    pooled = jnp.dot(masked.reshape(row_count // POOL, POOL * feature), pool_weight, preferred_element_type=jnp.float32)
    expanded = jax.nn.gelu(jnp.dot(normalize(fine), mlp_in, preferred_element_type=jnp.float32), approximate=True).astype(jnp.bfloat16)
    refined = fine.astype(jnp.float32) + jnp.dot(expanded, mlp_out, preferred_element_type=jnp.float32)
    return (pooled, refined)

def coarse_qkv(coarse_state, weights):
    normed = normalize(coarse_state)
    return (project(normed, weights[0]), project(normed, weights[1]), project(normed, weights[2]))

def coarse_update(coarse_state, queries, key_rows, value_rows, out_weight):
    mixed = attend(queries, key_rows, value_rows, None, HEADS)
    return coarse_state + jnp.dot(mixed, out_weight, preferred_element_type=jnp.float32)

def run_levels(coarse_state, coarse_proj, coarse_out, level_count):
    block_ids = np.arange(coarse_state.shape[0])
    for level_index in range(level_count):
        queries, key_rows, value_rows = coarse_qkv(coarse_state, coarse_proj)
        partner = block_ids ^ 1 << level_index
        coarse_state = coarse_update(coarse_state, queries, jnp.concatenate([key_rows, key_rows[partner]], axis=1), jnp.concatenate([value_rows, value_rows[partner]], axis=1), coarse_out)
    return coarse_state

def reference(points, tree_order, ball_counts, ball_proj, ball_out, pool_weight, coarse_proj, coarse_out, global_proj, global_out, unpool_weight, mlp_in, mlp_out):
    tree_rows = jnp.take(points, tree_order.astype(jnp.int32), axis=0)
    live_mask = (jnp.arange(BALL, dtype=jnp.int32)[None, :] < ball_counts[:, None]).reshape(-1)

    def one_block(pieces):
        return fine_section(pieces[0], pieces[1], ball_proj, ball_out, pool_weight, mlp_in, mlp_out)
    pooled, refined = lax.map(one_block, (tree_rows.reshape(N_POINT, TOK_DEV, D), live_mask.reshape(N_POINT, TOK_DEV)))
    coarse_state = run_levels(pooled, coarse_proj, coarse_out, LEVELS)
    queries, key_rows, value_rows = coarse_qkv(coarse_state, global_proj)
    mixed = attend(queries.reshape(1, COARSE, D), key_rows.reshape(1, COARSE, D), value_rows.reshape(1, COARSE, D), None, HEADS)
    summary = (coarse_state.reshape(1, COARSE, D) + jnp.dot(mixed, global_out, preferred_element_type=jnp.float32)).astype(jnp.bfloat16)
    unpooled = jnp.dot(summary.reshape(COARSE, D), unpool_weight, preferred_element_type=jnp.float32).reshape(TOKENS, D)
    total = refined.reshape(TOKENS, D) + unpooled
    return jnp.where(live_mask[:, None], total, 0.0).astype(jnp.bfloat16)
```

```python
import functools
import math

import jax
import jax.numpy as jnp
from jax import lax
from jax.experimental import pallas as pl
from jax.experimental.pallas import tpu as pltpu
from jax.sharding import PartitionSpec as P

HEADS = 8
BALL = 256
POOL = 64
EPSILON = 1e-05
F32 = jnp.float32
BF16 = jnp.bfloat16
MESH = pl.DeviceIdType.MESH
NT = (((1,), (1,)), ((), ()))
TN = (((0,), (0,)), ((), ()))


def normalize(inputs):
    center = inputs - jnp.mean(inputs, axis=-1, keepdims=True)
    spread = jnp.mean(center * center, axis=-1, keepdims=True)
    return (center * lax.rsqrt(spread + EPSILON)).astype(BF16)


def nt(a, b):
    return lax.dot_general(a, b, NT, preferred_element_type=F32)


def nn(a, b):
    return jnp.dot(a, b, preferred_element_type=F32)


def attend(q_in, kv_in, proj_ref, out_weight, valid):
    feature = q_in.shape[1]
    head = feature // HEADS
    rows, keys = q_in.shape[0], kv_in.shape[0]
    factor = math.log2(math.e) / math.sqrt(head)
    q_t = (nt(proj_ref[0], q_in) * factor).astype(BF16)
    k = nn(kv_in, proj_ref[1]).astype(BF16)
    v_t = nt(proj_ref[2], kv_in).astype(BF16)
    ones = jnp.ones((16, keys), BF16)
    outs = []
    for h in range(HEADS):
        lo, hi = h * head, (h + 1) * head
        parts = []
        if lo:
            parts.append(jnp.zeros((lo, rows), BF16))
        parts.append(q_t[lo:hi])
        if hi < feature:
            parts.append(jnp.zeros((feature - hi, rows), BF16))
        scores = nn(k, jnp.concatenate(parts, axis=0))
        if valid is not None:
            scores = jnp.where(valid, scores, -1e30)
        top = jnp.max(scores, axis=0, keepdims=True)
        expo = jnp.exp2(scores - top).astype(BF16)
        mixed = nn(jnp.concatenate([v_t[lo:hi], ones], axis=0), expo)
        outs.append((mixed[:head] * (1.0 / mixed[head : head + 1])).astype(BF16))
    return lax.dot_general(
        jnp.concatenate(outs, axis=0), out_weight, TN, preferred_element_type=F32
    )


def ball_kernel(
    order_ref, counts_ref, points_ref, proj_ref, out_ref, pool_ref,
    fine_ref, pooled_ref, wide, rows_ref, kept, pool_all,
):
    step = pl.program_id(0)
    steps = pl.num_programs(0)
    row_count = points_ref.shape[0]
    feature = points_ref.shape[1]
    pool_rows = pool_ref.shape[0]
    groups = row_count // POOL

    @pl.when(step == 0)
    def _():
        rows_ref[...] = jnp.zeros_like(rows_ref)

        def widen(t, carry):
            at = pl.ds(pl.multiple_of(t * BALL, BALL), BALL)
            wide[at, :] = points_ref[at, :].astype(F32)
            return carry

        lax.fori_loop(0, row_count // BALL, widen, 0)

    pool_all[pl.ds(pl.multiple_of(step * pool_rows, pool_rows), pool_rows), :] = pool_ref[...]
    count = counts_ref[step]
    first = step * BALL

    def take(g, carry):
        base = pl.multiple_of(g * 16, 16)
        for r in range(16):
            rows_ref[pl.ds(base + r, 1), :] = wide[pl.ds(order_ref[first + base + r], 1), :]
        return carry

    lax.fori_loop(0, (count + 15) // 16, take, 0)

    x = rows_ref[...]
    normed = normalize(x)
    valid = lax.broadcasted_iota(jnp.int32, (BALL, BALL), 0) < count
    fine = (x + attend(normed, normed, proj_ref, out_ref[...], valid)).astype(BF16)
    fine_ref[...] = fine
    live = lax.broadcasted_iota(jnp.int32, (BALL, feature), 0) < count
    at = pl.ds(pl.multiple_of(first, BALL), BALL)
    masked = jnp.where(live, fine.astype(F32), 0.0)
    for c in range(feature // 128):
        kept[c, at, :] = masked[:, c * 128 : (c + 1) * 128]

    @pl.when(step == steps - 1)
    def _():
        per = 8

        def pool(c, total):
            parts = []
            for r in range(per):
                for half in range(feature // 128):
                    parts.append(kept[half, pl.ds(c * per + r, groups, stride=POOL), :].astype(BF16))
            block = pl.ds(pl.multiple_of(c * (per * feature), per * feature), per * feature)
            return total + nn(jnp.concatenate(parts, axis=1), pool_all[block, :])

        total = lax.fori_loop(0, POOL // per, pool, jnp.zeros((groups, feature), F32))
        pooled_ref[...] = total.astype(BF16)


def ball_call(order, counts, points, proj, out_weight, pool_weight):
    row_count, feature = points.shape
    steps = row_count // BALL
    groups = row_count // POOL
    pool_rows = pool_weight.shape[0] // steps
    once = pl.Buffered(1)
    return pl.pallas_call(
        ball_kernel,
        grid_spec=pltpu.PrefetchScalarGridSpec(
            num_scalar_prefetch=2,
            grid=(steps,),
            in_specs=[
                pl.BlockSpec((row_count, feature), lambda i, *_: (0, 0), pipeline_mode=once),
                pl.BlockSpec(proj.shape, lambda i, *_: (0, 0, 0), pipeline_mode=once),
                pl.BlockSpec(out_weight.shape, lambda i, *_: (0, 0), pipeline_mode=once),
                pl.BlockSpec((pool_rows, feature), lambda i, *_: (i, 0)),
            ],
            out_specs=[
                pl.BlockSpec((BALL, feature), lambda i, *_: (i, 0)),
                pl.BlockSpec((groups, feature), lambda i, *_: (0, 0)),
            ],
            scratch_shapes=[
                pltpu.VMEM((row_count, feature), F32),
                pltpu.VMEM((BALL, feature), F32),
                pltpu.VMEM((feature // 128, row_count, 128), F32),
                pltpu.VMEM(pool_weight.shape, BF16),
            ],
        ),
        out_shape=[
            jax.ShapeDtypeStruct((row_count, feature), BF16),
            jax.ShapeDtypeStruct((groups, feature), BF16),
        ],
        compiler_params=pltpu.CompilerParams(vmem_limit_bytes=48 * 1024 * 1024),
        name="balls",
    )(order, counts, points, proj, out_weight, pool_weight)


def coarse_kernel(
    n, pooled_ref, fine_ref, cproj_ref, cout_ref, gproj_ref, gout_ref, win_ref, wout_ref,
    summary_ref, refined_ref, arrived, state, send_sem, recv_sem,
):
    me = lax.axis_index("point")
    tokens, feature = pooled_ref.shape
    row_count = fine_ref.shape[0]

    barrier = pltpu.get_barrier_semaphore()

    def greet(k, carry):
        peer = (me + k) % n
        pl.semaphore_signal(barrier, inc=1, device_id={"point": peer}, device_id_type=MESH)
        return carry

    lax.fori_loop(1, n, greet, 0)
    pl.semaphore_wait(barrier, n - 1)

    def copy_to(peer, slot, sender):
        return pltpu.make_async_remote_copy(
            src_ref=pooled_ref,
            dst_ref=arrived.at[sender],
            send_sem=send_sem.at[slot],
            recv_sem=recv_sem.at[sender],
            device_id={"point": peer},
            device_id_type=MESH,
        )

    def send(k, carry):
        copy_to((me + k) % n, k, me).start()
        return carry

    lax.fori_loop(1, n, send, 0)

    tile = 256

    def mlp(t, carry):
        at = pl.ds(pl.multiple_of(t * tile, tile), tile)
        fine = fine_ref[at, :].astype(F32)
        hidden = nn(normalize(fine), win_ref[...])
        expanded = jax.nn.gelu(hidden, approximate=True).astype(BF16)
        refined_ref[at, :] = (fine + nn(expanded, wout_ref[...])).astype(BF16)
        return carry

    lax.fori_loop(0, row_count // tile, mlp, 0)

    def land(k, carry):
        sender = (me + k) % n
        copy_to(sender, k, sender).wait_recv()
        state[pl.ds(pl.multiple_of(sender * tokens, tokens), tokens), :] = arrived[sender].astype(F32)
        return carry

    lax.fori_loop(1, n, land, 0)
    mine = pl.ds(pl.multiple_of(me * tokens, tokens), tokens)
    state[mine, :] = pooled_ref[...].astype(F32)

    apart = 1
    while apart < n:

        def pair(p, carry, apart=apart):
            low = (p // apart) * (2 * apart) + p % apart
            one = pl.ds(pl.multiple_of(low * tokens, tokens), tokens)
            two = pl.ds(pl.multiple_of((low + apart) * tokens, tokens), tokens)
            x = jnp.concatenate([state[one, :], state[two, :]], axis=0)
            normed = normalize(x)
            x = x + attend(normed, normed, cproj_ref, cout_ref[...], None)
            state[one, :] = x[:tokens]
            state[two, :] = x[tokens:]
            return carry

        lax.fori_loop(0, n // 2, pair, 0)
        apart *= 2

    x = state[mine, :]
    mixed = attend(normalize(x), normalize(state[...]), gproj_ref, gout_ref[...], None)
    summary_ref[...] = (x + mixed).astype(BF16)

    def sent(k, carry):
        copy_to((me + k) % n, k, me).wait_send()
        return carry

    lax.fori_loop(1, n, sent, 0)


def coarse_call(n, pooled, fine, cproj, cout, gproj, gout, mlp_in, mlp_out):
    tokens, feature = pooled.shape
    vmem = pl.BlockSpec(memory_space=pltpu.VMEM)
    return pl.pallas_call(
        functools.partial(coarse_kernel, n),
        in_specs=[vmem] * 8,
        out_specs=[vmem] * 2,
        out_shape=[
            jax.ShapeDtypeStruct((tokens, feature), BF16),
            jax.ShapeDtypeStruct(fine.shape, BF16),
        ],
        scratch_shapes=[
            pltpu.VMEM((n, tokens, feature), BF16),
            pltpu.VMEM((n * tokens, feature), F32),
            pltpu.SemaphoreType.DMA((n,)),
            pltpu.SemaphoreType.DMA((n,)),
        ],
        compiler_params=pltpu.CompilerParams(
            collective_id=0, has_side_effects=True, vmem_limit_bytes=40 * 1024 * 1024
        ),
        name="coarse",
    )(pooled, fine, cproj, cout, gproj, gout, mlp_in, mlp_out)


def unpool_kernel(half, counts_ref, summary_ref, weight_ref, refined_ref, out_ref, spread):
    step = pl.program_id(0)
    tokens, feature = summary_ref.shape
    per = weight_ref.shape[1] // feature
    rows = out_ref.shape[0]

    @pl.when(step < half)
    def _():
        for r in range(per):
            piece = nn(summary_ref[...], weight_ref[:, r * feature : (r + 1) * feature])
            for c in range(feature // 128):
                spread[c, pl.ds(step * per + r, tokens, stride=POOL), :] = piece[:, c * 128 : (c + 1) * 128]

    @pl.when(step >= half)
    def _():
        at = step - half
        for b in range(rows // BALL):
            here = slice(b * BALL, (b + 1) * BALL)
            count = counts_ref[at * (rows // BALL) + b]
            live = lax.broadcasted_iota(jnp.int32, (BALL, feature), 0) < count
            slots = pl.ds(pl.multiple_of(at * rows + b * BALL, BALL), BALL)
            wide = jnp.concatenate([spread[c, slots, :] for c in range(feature // 128)], axis=1)
            total = refined_ref[here, :].astype(F32) + wide
            out_ref[here, :] = jnp.where(live, total, 0.0).astype(BF16)


def unpool_call(counts, summary, weight, refined):
    row_count, feature = refined.shape
    half = 8
    rows = row_count // half
    columns = weight.shape[1] // half
    return pl.pallas_call(
        functools.partial(unpool_kernel, half),
        grid_spec=pltpu.PrefetchScalarGridSpec(
            num_scalar_prefetch=1,
            grid=(2 * half,),
            in_specs=[
                pl.BlockSpec(summary.shape, lambda i, *_: (0, 0)),
                pl.BlockSpec((feature, columns), lambda i, *_: (0, jnp.minimum(i, half - 1))),
                pl.BlockSpec((rows, feature), lambda i, *_: (jnp.maximum(i - half, 0), 0)),
            ],
            out_specs=pl.BlockSpec((rows, feature), lambda i, *_: (jnp.maximum(i - half, 0), 0)),
            scratch_shapes=[pltpu.VMEM((feature // 128, row_count, 128), F32)],
        ),
        out_shape=jax.ShapeDtypeStruct((row_count, feature), BF16),
        compiler_params=pltpu.CompilerParams(vmem_limit_bytes=32 * 1024 * 1024),
        name="unpool",
    )(counts, summary, weight, refined)


def turned(proj):
    return jnp.stack([proj[0].T, proj[1], proj[2].T])


def local(
    points, tree_order, ball_counts, ball_proj, ball_out, pool_weight, coarse_proj, coarse_out,
    global_proj, global_out, unpool_weight, mlp_in, mlp_out,
):
    n = lax.axis_size("point")
    order = tree_order - lax.axis_index("point") * points.shape[0]
    fine, pooled = ball_call(order, ball_counts, points, turned(ball_proj), ball_out, pool_weight)
    summary, refined = coarse_call(
        n, pooled, fine, turned(coarse_proj), coarse_out, turned(global_proj), global_out, mlp_in, mlp_out
    )
    return unpool_call(ball_counts, summary, unpool_weight, refined)


def solution(mesh):
    rows = P(("dp", "point"), None)
    line = P(("dp", "point"))
    return jax.shard_map(
        local,
        mesh=mesh,
        in_specs=(rows, line, line) + (P(),) * 10,
        out_specs=rows,
        check_vma=False,
    )
```

```python
import functools
import math

import jax
import jax.numpy as jnp
from jax import lax
from jax.experimental import pallas as pl
from jax.experimental.pallas import tpu as pltpu
from jax.sharding import PartitionSpec as P

HEADS = 8
BALL = 256
POOL = 64
EPSILON = 1e-05
F32 = jnp.float32
BF16 = jnp.bfloat16
MESH = pl.DeviceIdType.MESH
NT = (((1,), (1,)), ((), ()))
TN = (((0,), (0,)), ((), ()))


def normalize(inputs):
    center = inputs - jnp.mean(inputs, axis=-1, keepdims=True)
    spread = jnp.mean(center * center, axis=-1, keepdims=True)
    return (center * lax.rsqrt(spread + EPSILON)).astype(BF16)


def nt(a, b):
    return lax.dot_general(a, b, NT, preferred_element_type=F32)


def nn(a, b):
    return jnp.dot(a, b, preferred_element_type=F32)


def attend(q_in, kv_in, proj_ref, out_weight, count, between=None):
    feature = q_in.shape[1]
    head = feature // HEADS
    rows, keys = q_in.shape[0], kv_in.shape[0]
    factor = math.log2(math.e) / math.sqrt(head)
    q_t = (nt(proj_ref[0], q_in) * factor).astype(BF16)
    k = nn(kv_in, proj_ref[1]).astype(BF16)
    v_t = nt(proj_ref[2], kv_in).astype(BF16)
    ones = jnp.ones((16, keys), BF16)
    lane = lax.broadcasted_iota(jnp.int32, (1, feature), 1) // head
    valid = None
    if count is not None:
        valid = lax.broadcasted_iota(jnp.int32, (keys, rows), 0) < count
    outs = []
    together = 4
    for h0 in range(0, HEADS, together):
        own = [k * jnp.where(lane == h, 1.0, 0.0).astype(BF16) for h in range(h0, h0 + together)]
        all_scores = nn(jnp.concatenate(own, axis=0), q_t)
        for h in range(h0, h0 + together):
            lo, hi = h * head, (h + 1) * head
            scores = all_scores[(h - h0) * keys : (h - h0 + 1) * keys]
            if valid is not None:
                scores = jnp.where(valid, scores, -1e30)
            top = jnp.max(scores, axis=0, keepdims=True)
            expo = jnp.exp2((scores - top).astype(BF16))
            mixed = nn(jnp.concatenate([v_t[lo:hi], ones], axis=0), expo)
            outs.append((mixed[:head] * (1.0 / mixed[head : head + 1])).astype(BF16))
            if between is not None:
                between(h)
    return lax.dot_general(
        jnp.concatenate(outs, axis=0), out_weight, TN, preferred_element_type=F32
    )


def turn(proj_ref, turned_ref):
    turned_ref[0] = proj_ref[0].T
    turned_ref[1] = proj_ref[1]
    turned_ref[2] = proj_ref[2].T


def gelu(inputs):
    inner = inputs * (0.7978845608028654 + 0.035677408136300125 * (inputs * inputs))
    return inputs * (0.5 + 0.5 * jnp.tanh(inner))


def ball_kernel(
    order_ref, counts_ref, points_ref, proj_ref, out_ref, pool_ref,
    fine_ref, pooled_ref, wide, rows_ref, kept, pool_all, turned_ref,
):
    step = pl.program_id(0)
    steps = pl.num_programs(0)
    row_count = points_ref.shape[0]
    feature = points_ref.shape[1]
    pool_rows = pool_ref.shape[0]
    groups = row_count // POOL

    offset = lax.axis_index("point") * row_count

    def take(ball, slot, lo, hi):
        wanted = [
            wide[pl.ds(order_ref[ball * BALL + r] - offset, 1), :] for r in range(lo, hi)
        ]
        for r, row in zip(range(lo, hi), wanted):
            rows_ref[slot, r : r + 1, :] = row

    @pl.when(step == 0)
    def _():
        turn(proj_ref, turned_ref)

        def widen(t, carry):
            at = pl.ds(pl.multiple_of(t * BALL, BALL), BALL)
            wide[at, :] = points_ref[at, :].astype(F32)
            return carry

        lax.fori_loop(0, row_count // BALL, widen, 0)
        for lo in range(0, BALL, 16):
            take(0, 0, lo, lo + 16)

    pool_all[pl.ds(pl.multiple_of(step * pool_rows, pool_rows), pool_rows), :] = pool_ref[...]
    count = counts_ref[step]
    first = step * BALL
    slot = step % 2
    following = jnp.minimum(step + 1, steps - 1)
    share = BALL // HEADS

    def between(h):
        for lo in range(h * share, (h + 1) * share, 16):
            take(following, 1 - slot, lo, lo + 16)

    x = rows_ref[slot]
    normed = normalize(x)
    fine = (x + attend(normed, normed, turned_ref, out_ref[...], count, between)).astype(BF16)
    fine_ref[...] = fine
    live = lax.broadcasted_iota(jnp.int32, (BALL, feature), 0) < count
    at = pl.ds(pl.multiple_of(first, BALL), BALL)
    masked = jnp.where(live, fine.astype(F32), 0.0)
    for c in range(feature // 128):
        kept[c, at, :] = masked[:, c * 128 : (c + 1) * 128]

    @pl.when(step == steps - 1)
    def _():
        per = 8

        def pool(c, total):
            parts = []
            for r in range(per):
                for half in range(feature // 128):
                    parts.append(kept[half, pl.ds(c * per + r, groups, stride=POOL), :].astype(BF16))
            block = pl.ds(pl.multiple_of(c * (per * feature), per * feature), per * feature)
            return total + nn(jnp.concatenate(parts, axis=1), pool_all[block, :])

        total = lax.fori_loop(0, POOL // per, pool, jnp.zeros((groups, feature), F32))
        pooled_ref[...] = total.astype(BF16)


def ball_call(order, counts, points, proj, out_weight, pool_weight):
    row_count, feature = points.shape
    steps = row_count // BALL
    groups = row_count // POOL
    pool_rows = pool_weight.shape[0] // steps
    once = pl.Buffered(1)
    return pl.pallas_call(
        ball_kernel,
        grid_spec=pltpu.PrefetchScalarGridSpec(
            num_scalar_prefetch=2,
            grid=(steps,),
            in_specs=[
                pl.BlockSpec((row_count, feature), lambda i, *_: (0, 0), pipeline_mode=once),
                pl.BlockSpec(proj.shape, lambda i, *_: (0, 0, 0), pipeline_mode=once),
                pl.BlockSpec(out_weight.shape, lambda i, *_: (0, 0), pipeline_mode=once),
                pl.BlockSpec((pool_rows, feature), lambda i, *_: (i, 0)),
            ],
            out_specs=[
                pl.BlockSpec((BALL, feature), lambda i, *_: (i, 0)),
                pl.BlockSpec((groups, feature), lambda i, *_: (0, 0)),
            ],
            scratch_shapes=[
                pltpu.VMEM((row_count, feature), F32),
                pltpu.VMEM((2, BALL, feature), F32),
                pltpu.VMEM((feature // 128, row_count, 128), F32),
                pltpu.VMEM(pool_weight.shape, BF16),
                pltpu.VMEM(proj.shape, BF16),
            ],
        ),
        out_shape=[
            jax.ShapeDtypeStruct((row_count, feature), BF16),
            jax.ShapeDtypeStruct((groups, feature), BF16),
        ],
        compiler_params=pltpu.CompilerParams(vmem_limit_bytes=48 * 1024 * 1024),
        name="balls",
    )(order, counts, points, proj, out_weight, pool_weight)


def coarse_kernel(
    n, pooled_ref, fine_ref, cproj_ref, cout_ref, gproj_ref, gout_ref, win_ref, wout_ref,
    summary_ref, refined_ref, arrived, state, cturned, gturned, send_sem, recv_sem,
):
    me = lax.axis_index("point")
    tokens, feature = pooled_ref.shape
    row_count = fine_ref.shape[0]

    barrier = pltpu.get_barrier_semaphore()

    def greet(k, carry):
        peer = (me + k) % n
        pl.semaphore_signal(barrier, inc=1, device_id={"point": peer}, device_id_type=MESH)
        return carry

    lax.fori_loop(1, n, greet, 0)
    turn(cproj_ref, cturned)
    turn(gproj_ref, gturned)
    pl.semaphore_wait(barrier, n - 1)

    def copy_to(peer, slot, sender):
        return pltpu.make_async_remote_copy(
            src_ref=pooled_ref,
            dst_ref=arrived.at[sender],
            send_sem=send_sem.at[slot],
            recv_sem=recv_sem.at[sender],
            device_id={"point": peer},
            device_id_type=MESH,
        )

    def send(k, carry):
        copy_to((me + k) % n, k, me).start()
        return carry

    lax.fori_loop(1, n, send, 0)

    tile = 256

    def mlp(t, carry):
        for u in range(2):
            at = pl.ds(pl.multiple_of((t * 2 + u) * tile, tile), tile)
            fine = fine_ref[at, :].astype(F32)
            hidden = nn(normalize(fine), win_ref[...]).astype(BF16)
            refined_ref[at, :] = (fine + nn(gelu(hidden), wout_ref[...])).astype(BF16)
        return carry

    lax.fori_loop(0, row_count // (2 * tile), mlp, 0)

    def land(k, carry):
        sender = (me + k) % n
        copy_to(sender, k, sender).wait_recv()
        state[pl.ds(pl.multiple_of(sender * tokens, tokens), tokens), :] = arrived[sender].astype(F32)
        return carry

    lax.fori_loop(1, n, land, 0)
    mine = pl.ds(pl.multiple_of(me * tokens, tokens), tokens)
    state[mine, :] = pooled_ref[...].astype(F32)

    apart = 1
    while apart < n:

        def couple(p, apart=apart):
            low = (p // apart) * (2 * apart) + p % apart
            one = pl.ds(pl.multiple_of(low * tokens, tokens), tokens)
            two = pl.ds(pl.multiple_of((low + apart) * tokens, tokens), tokens)
            x = jnp.concatenate([state[one, :], state[two, :]], axis=0)
            normed = normalize(x)
            x = x + attend(normed, normed, cturned, cout_ref[...], None)
            return one, two, x

        def pairs(p, carry, couple=couple):
            done = [couple(2 * p), couple(2 * p + 1)]
            for one, two, x in done:
                state[one, :] = x[:tokens]
                state[two, :] = x[tokens:]
            return carry

        lax.fori_loop(0, n // 4, pairs, 0)
        apart *= 2

    x = state[mine, :]
    mixed = attend(normalize(x), normalize(state[...]), gturned, gout_ref[...], None)
    summary_ref[...] = (x + mixed).astype(BF16)

    def sent(k, carry):
        copy_to((me + k) % n, k, me).wait_send()
        return carry

    lax.fori_loop(1, n, sent, 0)


def coarse_call(n, pooled, fine, cproj, cout, gproj, gout, mlp_in, mlp_out):
    tokens, feature = pooled.shape
    vmem = pl.BlockSpec(memory_space=pltpu.VMEM)
    return pl.pallas_call(
        functools.partial(coarse_kernel, n),
        in_specs=[vmem] * 8,
        out_specs=[vmem] * 2,
        out_shape=[
            jax.ShapeDtypeStruct((tokens, feature), BF16),
            jax.ShapeDtypeStruct(fine.shape, BF16),
        ],
        scratch_shapes=[
            pltpu.VMEM((n, tokens, feature), BF16),
            pltpu.VMEM((n * tokens, feature), F32),
            pltpu.VMEM(cproj.shape, BF16),
            pltpu.VMEM(gproj.shape, BF16),
            pltpu.SemaphoreType.DMA((n,)),
            pltpu.SemaphoreType.DMA((n,)),
        ],
        compiler_params=pltpu.CompilerParams(
            collective_id=0, has_side_effects=True, vmem_limit_bytes=40 * 1024 * 1024
        ),
        name="coarse",
    )(pooled, fine, cproj, cout, gproj, gout, mlp_in, mlp_out)


def unpool_kernel(half, counts_ref, summary_ref, weight_ref, refined_ref, out_ref, spread):
    step = pl.program_id(0)
    tokens, feature = summary_ref.shape
    per = weight_ref.shape[1] // feature
    rows = out_ref.shape[0]

    @pl.when(step < half)
    def _():
        for r in range(per):
            piece = nn(summary_ref[...], weight_ref[:, r * feature : (r + 1) * feature])
            for c in range(feature // 128):
                spread[c, pl.ds(step * per + r, tokens, stride=POOL), :] = piece[:, c * 128 : (c + 1) * 128]

    @pl.when(step >= half)
    def _():
        at = step - half
        for b in range(rows // BALL):
            here = slice(b * BALL, (b + 1) * BALL)
            count = counts_ref[at * (rows // BALL) + b]
            live = lax.broadcasted_iota(jnp.int32, (BALL, feature), 0) < count
            slots = pl.ds(pl.multiple_of(at * rows + b * BALL, BALL), BALL)
            wide = jnp.concatenate([spread[c, slots, :] for c in range(feature // 128)], axis=1)
            total = refined_ref[here, :].astype(F32) + wide
            out_ref[here, :] = jnp.where(live, total, 0.0).astype(BF16)


def unpool_call(counts, summary, weight, refined):
    row_count, feature = refined.shape
    half = 8
    rows = row_count // half
    columns = weight.shape[1] // half
    return pl.pallas_call(
        functools.partial(unpool_kernel, half),
        grid_spec=pltpu.PrefetchScalarGridSpec(
            num_scalar_prefetch=1,
            grid=(2 * half,),
            in_specs=[
                pl.BlockSpec(summary.shape, lambda i, *_: (0, 0)),
                pl.BlockSpec((feature, columns), lambda i, *_: (0, jnp.minimum(i, half - 1))),
                pl.BlockSpec((rows, feature), lambda i, *_: (jnp.maximum(i - half, 0), 0)),
            ],
            out_specs=pl.BlockSpec((rows, feature), lambda i, *_: (jnp.maximum(i - half, 0), 0)),
            scratch_shapes=[pltpu.VMEM((feature // 128, row_count, 128), F32)],
        ),
        out_shape=jax.ShapeDtypeStruct((row_count, feature), BF16),
        compiler_params=pltpu.CompilerParams(vmem_limit_bytes=32 * 1024 * 1024),
        name="unpool",
    )(counts, summary, weight, refined)


def local(
    points, tree_order, ball_counts, ball_proj, ball_out, pool_weight, coarse_proj, coarse_out,
    global_proj, global_out, unpool_weight, mlp_in, mlp_out,
):
    n = lax.axis_size("point")
    fine, pooled = ball_call(tree_order, ball_counts, points, ball_proj, ball_out, pool_weight)
    summary, refined = coarse_call(
        n, pooled, fine, coarse_proj, coarse_out, global_proj, global_out, mlp_in, mlp_out
    )
    return unpool_call(ball_counts, summary, unpool_weight, refined)


def solution(mesh):
    rows = P(("dp", "point"), None)
    line = P(("dp", "point"))
    return jax.shard_map(
        local,
        mesh=mesh,
        in_specs=(rows, line, line) + (P(),) * 10,
        out_specs=rows,
        check_vma=False,
    )
```

```python
import functools
import math

import jax
import jax.numpy as jnp
from jax import lax
from jax.experimental import pallas as pl
from jax.experimental.pallas import tpu as pltpu
from jax.sharding import PartitionSpec as P

HEADS = 8
BALL = 256
POOL = 64
EPSILON = 1e-05
F32 = jnp.float32
BF16 = jnp.bfloat16
MESH = pl.DeviceIdType.MESH
NT = (((1,), (1,)), ((), ()))
TN = (((0,), (0,)), ((), ()))


def normalize(inputs):
    center = inputs - jnp.mean(inputs, axis=-1, keepdims=True)
    spread = jnp.mean(center * center, axis=-1, keepdims=True)
    return (center * lax.rsqrt(spread + EPSILON)).astype(BF16)


def nt(a, b):
    return lax.dot_general(a, b, NT, preferred_element_type=F32)


def nn(a, b):
    return jnp.dot(a, b, preferred_element_type=F32)


def attend(q_in, kv_in, proj_ref, out_weight, count, between=None):
    feature = q_in.shape[1]
    head = feature // HEADS
    rows, keys = q_in.shape[0], kv_in.shape[0]
    factor = math.log2(math.e) / math.sqrt(head)
    q_t = (nt(proj_ref[0], q_in) * factor).astype(BF16)
    k = nn(kv_in, proj_ref[1]).astype(BF16)
    v_t = nt(proj_ref[2], kv_in).astype(BF16)
    ones = jnp.ones((16, keys), BF16)
    lane = lax.broadcasted_iota(jnp.int32, (1, feature), 1) // head
    valid = None
    if count is not None:
        valid = lax.broadcasted_iota(jnp.int32, (keys, rows), 0) < count
    outs = []
    together = 4
    for h0 in range(0, HEADS, together):
        own = [k * jnp.where(lane == h, 1.0, 0.0).astype(BF16) for h in range(h0, h0 + together)]
        all_scores = nn(jnp.concatenate(own, axis=0), q_t)
        for h in range(h0, h0 + together):
            lo, hi = h * head, (h + 1) * head
            scores = all_scores[(h - h0) * keys : (h - h0 + 1) * keys]
            if valid is not None:
                scores = jnp.where(valid, scores, -1e30)
            top = jnp.max(scores, axis=0, keepdims=True)
            expo = jnp.exp2((scores - top).astype(BF16))
            mixed = nn(jnp.concatenate([v_t[lo:hi], ones], axis=0), expo)
            outs.append((mixed[:head] * (1.0 / mixed[head : head + 1])).astype(BF16))
            if between is not None:
                between(h)
    return lax.dot_general(
        jnp.concatenate(outs, axis=0), out_weight, TN, preferred_element_type=F32
    )


def turn(proj_ref, turned_ref):
    turned_ref[0] = proj_ref[0].T
    turned_ref[1] = proj_ref[1]
    turned_ref[2] = proj_ref[2].T


def gelu(inputs):
    inner = inputs * (0.7978845608028654 + 0.035677408136300125 * (inputs * inputs))
    return inputs * (0.5 + 0.5 * jnp.tanh(inner))


def ball_kernel(
    order_ref, counts_ref, points_ref, proj_ref, out_ref, win_ref, wout_ref, pool_ref,
    refined_ref, pooled_ref, wide, rows_ref, kept, pool_all, turned_ref, before,
):
    step = pl.program_id(0)
    steps = pl.num_programs(0)
    row_count = points_ref.shape[0]
    feature = points_ref.shape[1]
    pool_rows = pool_ref.shape[0]
    groups = row_count // POOL

    offset = lax.axis_index("point") * row_count

    def take(ball, slot, lo, hi):
        wanted = [
            wide[pl.ds(order_ref[ball * BALL + r] - offset, 1), :] for r in range(lo, hi)
        ]
        for r, row in zip(range(lo, hi), wanted):
            rows_ref[slot, r : r + 1, :] = row

    @pl.when(step == 0)
    def _():
        turn(proj_ref, turned_ref)
        before[...] = jnp.zeros_like(before)

        def widen(t, carry):
            at = pl.ds(pl.multiple_of(t * BALL, BALL), BALL)
            wide[at, :] = points_ref[at, :].astype(F32)
            return carry

        lax.fori_loop(0, row_count // BALL, widen, 0)
        for lo in range(0, BALL, 16):
            take(0, 0, lo, lo + 16)

    piece = jnp.minimum(step, steps - 2)
    pool_all[pl.ds(pl.multiple_of(piece * pool_rows, pool_rows), pool_rows), :] = pool_ref[...]
    last = steps - 1
    ball = jnp.minimum(step, last - 1)
    count = counts_ref[ball]
    first = ball * BALL
    slot = step % 2
    following = jnp.minimum(step + 1, last - 1)
    share = BALL // HEADS
    width = win_ref.shape[1] // 4

    def mlp_parts():
        fine = before[...]
        normed = normalize(fine)
        total = [fine]

        def part(c):
            columns = slice(c * width, (c + 1) * width)
            hidden = nn(normed, win_ref[:, columns]).astype(BF16)
            total[0] = total[0] + nn(gelu(hidden), wout_ref[columns, :])

        def end():
            refined_ref[...] = total[0].astype(BF16)

        return part, end

    def run(keys, rows):
        part, end = mlp_parts()

        def between(h):
            for lo in range(h * share, (h + 1) * share, 16):
                take(following, 1 - slot, lo, lo + 16)
            if h % 2 == 0:
                part(h // 2)

        x = rows_ref[slot, :rows, :]
        normed = normalize(x)
        mixed = attend(normed, normed[:keys], turned_ref, out_ref[...], count, between)
        end()
        fine = (x + mixed).astype(BF16).astype(F32)
        live = lax.broadcasted_iota(jnp.int32, (rows, feature), 0) < count
        masked = jnp.where(live, fine, 0.0)
        before[:rows, :] = fine
        at = pl.ds(pl.multiple_of(first, BALL), rows)
        for c in range(feature // 128):
            kept[c, at, :] = masked[:, c * 128 : (c + 1) * 128]
        if rows < BALL:
            before[rows:, :] = jnp.zeros((BALL - rows, feature), F32)
            rest = pl.ds(pl.multiple_of(first + rows, 128), BALL - rows)
            for c in range(feature // 128):
                kept[c, rest, :] = jnp.zeros((BALL - rows, 128), F32)

    balls_left = step < last

    @pl.when(jnp.logical_and(balls_left, count <= 128))
    def _():
        run(128, 128)

    @pl.when(jnp.logical_and(balls_left, jnp.logical_and(count > 128, count <= 192)))
    def _():
        run(192, BALL)

    @pl.when(jnp.logical_and(balls_left, count > 192))
    def _():
        run(BALL, BALL)

    @pl.when(step == last)
    def _():
        part, end = mlp_parts()
        for c in range(4):
            part(c)
        end()
        per = 8

        def pool(c, total):
            parts = []
            for r in range(per):
                for half in range(feature // 128):
                    parts.append(kept[half, pl.ds(c * per + r, groups, stride=POOL), :].astype(BF16))
            block = pl.ds(pl.multiple_of(c * (per * feature), per * feature), per * feature)
            return total + nn(jnp.concatenate(parts, axis=1), pool_all[block, :])

        total = lax.fori_loop(0, POOL // per, pool, jnp.zeros((groups, feature), F32))
        pooled_ref[...] = total.astype(BF16)


def ball_call(order, counts, points, proj, out_weight, mlp_in, mlp_out, pool_weight):
    row_count, feature = points.shape
    steps = row_count // BALL
    groups = row_count // POOL
    pool_rows = pool_weight.shape[0] // steps
    once = pl.Buffered(1)
    return pl.pallas_call(
        ball_kernel,
        grid_spec=pltpu.PrefetchScalarGridSpec(
            num_scalar_prefetch=2,
            grid=(steps + 1,),
            in_specs=[
                pl.BlockSpec((row_count, feature), lambda i, *_: (0, 0), pipeline_mode=once),
                pl.BlockSpec(proj.shape, lambda i, *_: (0, 0, 0), pipeline_mode=once),
                pl.BlockSpec(out_weight.shape, lambda i, *_: (0, 0), pipeline_mode=once),
                pl.BlockSpec(mlp_in.shape, lambda i, *_: (0, 0), pipeline_mode=once),
                pl.BlockSpec(mlp_out.shape, lambda i, *_: (0, 0), pipeline_mode=once),
                pl.BlockSpec((pool_rows, feature), lambda i, *_: (jnp.minimum(i, steps - 1), 0)),
            ],
            out_specs=[
                pl.BlockSpec((BALL, feature), lambda i, *_: (jnp.maximum(i - 1, 0), 0)),
                pl.BlockSpec((groups, feature), lambda i, *_: (0, 0)),
            ],
            scratch_shapes=[
                pltpu.VMEM((row_count, feature), F32),
                pltpu.VMEM((2, BALL, feature), F32),
                pltpu.VMEM((feature // 128, row_count, 128), F32),
                pltpu.VMEM(pool_weight.shape, BF16),
                pltpu.VMEM(proj.shape, BF16),
                pltpu.VMEM((BALL, feature), F32),
            ],
        ),
        out_shape=[
            jax.ShapeDtypeStruct((row_count, feature), BF16),
            jax.ShapeDtypeStruct((groups, feature), BF16),
        ],
        compiler_params=pltpu.CompilerParams(vmem_limit_bytes=58 * 1024 * 1024),
        name="balls",
    )(order, counts, points, proj, out_weight, mlp_in, mlp_out, pool_weight)


def coarse_kernel(
    n, pooled_ref, cproj_ref, cout_ref, gproj_ref, gout_ref, summary_ref, arrived, state, cturned, gturned, send_sem, recv_sem,
):
    me = lax.axis_index("point")
    tokens, feature = pooled_ref.shape

    barrier = pltpu.get_barrier_semaphore()

    def greet(k, carry):
        peer = (me + k) % n
        pl.semaphore_signal(barrier, inc=1, device_id={"point": peer}, device_id_type=MESH)
        return carry

    lax.fori_loop(1, n, greet, 0)
    pl.semaphore_wait(barrier, n - 1)

    def copy_to(peer, slot, sender):
        return pltpu.make_async_remote_copy(
            src_ref=pooled_ref,
            dst_ref=arrived.at[sender],
            send_sem=send_sem.at[slot],
            recv_sem=recv_sem.at[sender],
            device_id={"point": peer},
            device_id_type=MESH,
        )

    def send(k, carry):
        copy_to((me + k) % n, k, me).start()
        return carry

    lax.fori_loop(1, n, send, 0)
    turn(cproj_ref, cturned)
    turn(gproj_ref, gturned)

    def land(k, carry):
        sender = (me + k) % n
        copy_to(sender, k, sender).wait_recv()
        state[pl.ds(pl.multiple_of(sender * tokens, tokens), tokens), :] = arrived[sender].astype(F32)
        return carry

    lax.fori_loop(1, n, land, 0)
    mine = pl.ds(pl.multiple_of(me * tokens, tokens), tokens)
    state[mine, :] = pooled_ref[...].astype(F32)

    apart = 1
    while apart < n:

        def couple(p, apart=apart):
            low = (p // apart) * (2 * apart) + p % apart
            one = pl.ds(pl.multiple_of(low * tokens, tokens), tokens)
            two = pl.ds(pl.multiple_of((low + apart) * tokens, tokens), tokens)
            x = jnp.concatenate([state[one, :], state[two, :]], axis=0)
            normed = normalize(x)
            x = x + attend(normed, normed, cturned, cout_ref[...], None)
            return one, two, x

        def pairs(p, carry, couple=couple):
            done = [couple(2 * p), couple(2 * p + 1)]
            for one, two, x in done:
                state[one, :] = x[:tokens]
                state[two, :] = x[tokens:]
            return carry

        lax.fori_loop(0, n // 4, pairs, 0)
        apart *= 2

    x = state[mine, :]
    mixed = attend(normalize(x), normalize(state[...]), gturned, gout_ref[...], None)
    summary_ref[...] = (x + mixed).astype(BF16)

    def sent(k, carry):
        copy_to((me + k) % n, k, me).wait_send()
        return carry

    lax.fori_loop(1, n, sent, 0)


def coarse_call(n, pooled, cproj, cout, gproj, gout):
    tokens, feature = pooled.shape
    vmem = pl.BlockSpec(memory_space=pltpu.VMEM)
    return pl.pallas_call(
        functools.partial(coarse_kernel, n),
        in_specs=[vmem] * 5,
        out_specs=vmem,
        out_shape=jax.ShapeDtypeStruct((tokens, feature), BF16),
        scratch_shapes=[
            pltpu.VMEM((n, tokens, feature), BF16),
            pltpu.VMEM((n * tokens, feature), F32),
            pltpu.VMEM(cproj.shape, BF16),
            pltpu.VMEM(gproj.shape, BF16),
            pltpu.SemaphoreType.DMA((n,)),
            pltpu.SemaphoreType.DMA((n,)),
        ],
        compiler_params=pltpu.CompilerParams(
            collective_id=0, has_side_effects=True, vmem_limit_bytes=32 * 1024 * 1024
        ),
        name="coarse",
    )(pooled, cproj, cout, gproj, gout)


def unpool_kernel(half, counts_ref, summary_ref, weight_ref, refined_ref, out_ref, spread):
    step = pl.program_id(0)
    tokens, feature = summary_ref.shape
    per = weight_ref.shape[1] // feature
    rows = out_ref.shape[0]

    @pl.when(step < half)
    def _():
        for r in range(per):
            piece = nn(summary_ref[...], weight_ref[:, r * feature : (r + 1) * feature])
            for c in range(feature // 128):
                spread[c, pl.ds(step * per + r, tokens, stride=POOL), :] = piece[:, c * 128 : (c + 1) * 128]

    @pl.when(step >= half)
    def _():
        at = step - half
        for b in range(rows // BALL):
            here = slice(b * BALL, (b + 1) * BALL)
            count = counts_ref[at * (rows // BALL) + b]
            live = lax.broadcasted_iota(jnp.int32, (BALL, feature), 0) < count
            slots = pl.ds(pl.multiple_of(at * rows + b * BALL, BALL), BALL)
            wide = jnp.concatenate([spread[c, slots, :] for c in range(feature // 128)], axis=1)
            total = refined_ref[here, :].astype(F32) + wide
            out_ref[here, :] = jnp.where(live, total, 0.0).astype(BF16)


def unpool_call(counts, summary, weight, refined):
    row_count, feature = refined.shape
    half = 8
    rows = row_count // half
    columns = weight.shape[1] // half
    return pl.pallas_call(
        functools.partial(unpool_kernel, half),
        grid_spec=pltpu.PrefetchScalarGridSpec(
            num_scalar_prefetch=1,
            grid=(2 * half,),
            in_specs=[
                pl.BlockSpec(summary.shape, lambda i, *_: (0, 0)),
                pl.BlockSpec((feature, columns), lambda i, *_: (0, jnp.minimum(i, half - 1))),
                pl.BlockSpec((rows, feature), lambda i, *_: (jnp.maximum(i - half, 0), 0)),
            ],
            out_specs=pl.BlockSpec((rows, feature), lambda i, *_: (jnp.maximum(i - half, 0), 0)),
            scratch_shapes=[pltpu.VMEM((feature // 128, row_count, 128), F32)],
        ),
        out_shape=jax.ShapeDtypeStruct((row_count, feature), BF16),
        compiler_params=pltpu.CompilerParams(vmem_limit_bytes=24 * 1024 * 1024),
        name="unpool",
    )(counts, summary, weight, refined)


def local(
    points, tree_order, ball_counts, ball_proj, ball_out, pool_weight, coarse_proj, coarse_out,
    global_proj, global_out, unpool_weight, mlp_in, mlp_out,
):
    n = lax.axis_size("point")
    refined, pooled = ball_call(
        tree_order, ball_counts, points, ball_proj, ball_out, mlp_in, mlp_out, pool_weight
    )
    summary = coarse_call(n, pooled, coarse_proj, coarse_out, global_proj, global_out)
    return unpool_call(ball_counts, summary, unpool_weight, refined)


def solution(mesh):
    rows = P(("dp", "point"), None)
    line = P(("dp", "point"))
    return jax.shard_map(
        local,
        mesh=mesh,
        in_specs=(rows, line, line) + (P(),) * 10,
        out_specs=rows,
        check_vma=False,
    )
```
